32 devices in a mesh: expert: 16 (over z, y, x), tensor: 2 (over core).
Axes of the slice: x: 2, y: 2, z: 4, core: 2. Of those that a mesh axis runs over, the one named last changes fastest.
Arguments:
- attn_parts: bfloat16 [2, 2048, 4096], P('tensor', 'expert'), may hold values from -4 to 4
- resid: bfloat16 [2048, 4096], P('expert', 'tensor'), may hold values from -48 to 48
- norm_gain: float32 [4096], P('tensor'), may hold values from 0.1 to 1.9
- w_gate: bfloat16 [16, 4096, 768], P('expert', 'tensor'), may hold values from -0.09375 to 0.09375
- w_up: bfloat16 [16, 4096, 768], P('expert', 'tensor'), may hold values from -0.09375 to 0.09375
- w_down: bfloat16 [16, 768, 4096], P('expert', None, 'tensor'), may hold values from -0.21875 to 0.21875
- expert_ids: int32 [2048, 4], P('expert'), may hold values from 0 to 15, all different within a row; in each aligned block of 128 rows (0 to 127, 128 to 255, ...) at most 40 rows name the same one
- gate_weights: float32 [2048, 4], P('expert'), may hold values from 0.1 to 1
- grad_out: bfloat16 [2048, 4096], P('expert', 'tensor'), may hold values from -6 to 6
Outputs:
- output: bfloat16 [2048, 4096], P('expert', 'tensor')
- grad_input: bfloat16 [2048, 4096], P('expert', 'tensor')
The draws below stay inside these ranges and needn't reach their ends.
Inputs may be any that keep to these rules, and one draw needn't show every extreme that they name: `expert_ids`: each row names 4 different experts. In each aligned block of 128 rows (the tokens of one group) no expert is named by more than 40 rows, a bound that some block reaches.
All inputs are finite; a program needn't handle non-finite values.
Results may differ from the reference program's by a relative error of at most 0.014.
Values may be sent and summed in bfloat16 or wider, within the bound.
A program may use at most 128 MiB of HBM per device.

```python
import math
import jax
import jax.numpy as jnp
import numpy as np
from jax import lax

D = 4096
FFN = 768
TOPK = 4
TOK = 128
EXPERTS = 16
CAP = 40
TOKENS = 2048
N_TENSOR = 2


def draw_resid(key, part):
    base_key, rough_key, row_key = jax.random.split(key, 3)
    column_place = jnp.arange(D, dtype=jnp.float32) / D
    column_scale = jnp.exp(math.log(0.3) + column_place * math.log(10.0))
    column_scale = column_scale * jax.random.uniform(rough_key, (D,), jnp.float32, 0.7, 1.3)
    row_scale = jnp.exp(jax.random.uniform(row_key, (TOKENS, 1), jnp.float32, math.log(0.2), math.log(2.0)))
    values = jnp.clip(jax.random.normal(base_key, (TOKENS, D), jnp.float32), -6.0, 6.0)
    return (values * column_scale[None, :] * row_scale).astype(jnp.bfloat16)


def spiked(drawn, stream_key, source, target, parts, factor):
    def block_of(axis_at):
        return (jnp.arange(drawn.shape[axis_at]) // (drawn.shape[axis_at] // parts)).reshape((-1,) + (1,) * (drawn.ndim - 1 - axis_at))

    first = jax.random.permutation(stream_key, parts)[block_of(target)]
    second = (block_of(target) + parts // 2) % parts
    return jnp.where((block_of(source) == first) | (block_of(source) == second), factor * drawn, drawn)


def levels(own_key, dims, pieces, smallest, top_value):
    def one(dim, shards_of):
        steps = jax.random.uniform(jax.random.fold_in(jax.random.fold_in(own_key, 6), dim), (shards_of,), jnp.float32, smallest / len(pieces), top_value / len(pieces))
        return jnp.repeat(jnp.exp(steps), dims[dim] // shards_of).reshape((-1,) + (1,) * (len(dims) - dim - 1))

    level = one(*pieces[0])
    for cut in pieces[1:]:
        level = level * one(*cut)
    return level


def assign_block(own_key, own, number, rows, count, top, limit, lean):
    order = jax.random.permutation(own_key, count)
    heavy_load, common = load_shares(count, rows * top, limit, lean, True), load_shares(count, rows * top, limit, lean, False)
    places = jnp.arange(count)

    def named(sizes, offset_by):
        used = int((sizes > 0).sum())
        fixed = max(1, used // 4)
        shifted = fixed + (places - fixed + offset_by * (used - fixed)) % max(1, count - fixed)
        return jnp.zeros((count,), jnp.int32).at[order[jnp.where(places < fixed, places, shifted)]].set(jnp.asarray(sizes, jnp.int32))

    sizes = jnp.where(number % 4 == 0, named(heavy_load, number // 4), named(common, number - number // 4 - 1))
    mixed = jax.random.permutation(jax.random.fold_in(own, 3), count)
    donor, receiver = mixed[0:count // 2 * 2:2], mixed[1:count // 2 * 2:2]
    room = jnp.minimum(sizes[donor] - 1, limit - sizes[receiver]) // 2
    room = jnp.where((donor == order[0]) | (receiver == order[0]) | (sizes[receiver] == 0), 0, jnp.maximum(room, 0))
    shifted = jax.random.randint(jax.random.fold_in(own, 4), (count // 2,), 0, 1 << 20) % (room + 1)
    sizes = sizes.at[donor].add(-shifted).at[receiver].add(shifted)
    members = jnp.searchsorted(jnp.cumsum(sizes), jnp.arange(rows * top), side="right").astype(jnp.int32)
    table = members.reshape(top, rows).T
    table = table[jax.random.permutation(jax.random.fold_in(own, 1), rows)]
    offset_by = jax.random.randint(jax.random.fold_in(own, 2), (rows, 1), 0, top)
    return jnp.take_along_axis(table, (jnp.arange(top)[None, :] + offset_by) % top, axis=1)


def load_shares(amount, total, bound, slope, full):
    portions = [(1 << 20) // math.isqrt(rank ** slope) + 1 for rank in range(1, amount + 1)]
    largest = bound if full else min(bound, max(-(-total // amount), total * portions[0] // sum(portions)))
    least = 1 if total - largest >= amount - 1 else 0
    holding, spare = [largest] + [least] * (amount - 1), total - largest - least * (amount - 1)
    while spare > 0:
        candidates = [i for i in range(1, amount) if holding[i] < largest] or [i for i in range(1, amount) if holding[i] < bound]
        mass, remaining = sum([portions[i] for i in candidates]), spare
        for i in candidates:
            extra = min(bound - holding[i], max(1, remaining * portions[i] // mass), spare)
            holding[i] = holding[i] + extra
            spare = spare - extra
    return np.array(holding)


def bell_draw(own_key, dims, spread, reach, cuts=(), kind=jnp.bfloat16):
    result = jax.random.normal(own_key, dims, jnp.float32) * spread
    if len(cuts) > 0:
        result = levels(own_key, dims, cuts, -0.22, 0.18) * result
    return jnp.clip(result, min=-reach, max=reach).astype(kind)


def gaussian_with(own_key, extent, width, limit, cuts, heavy, kind=jnp.bfloat16):
    drawn = width * jax.random.normal(own_key, extent, jnp.float32)
    if cuts:
        drawn = drawn * levels(own_key, extent, cuts, -0.22, 0.18)
    return jnp.clip(spiked(drawn, jax.random.fold_in(own_key, 3), *heavy), -limit, limit).astype(kind)


def setup_inputs(seed: int = 0) -> dict:
    key_of = jax.random.split(jax.random.key(seed), 10)
    attn_parts = gaussian_with(key_of[0], (N_TENSOR, TOKENS, D), 0.5, 4.0, ((0, 2), (1, 16)), (0, 2, 2, 2.0))
    resid = draw_resid(jax.random.fold_in(key_of[9], 71), 0)
    norm_gain = jnp.clip(1.0 + 0.18 * jax.random.normal(key_of[2], (D,), jnp.float32), 0.1, 1.9)
    w_gate = bell_draw(key_of[3], (EXPERTS, D, FFN), D ** -0.5, 0.09375, ((0, 16), (1, 2)))
    w_up = bell_draw(key_of[4], (EXPERTS, D, FFN), D ** -0.5, 0.09375, ((0, 16), (1, 2)))
    w_down = bell_draw(key_of[5], (EXPERTS, FFN, D), FFN ** -0.5, 0.21875, ((0, 16), (2, 2)))
    expert_ids_keys = jax.random.split(jax.random.fold_in(key_of[6], 1), TOKENS // TOK)
    expert_ids_turns = jax.random.permutation(jax.random.fold_in(key_of[6], 3), TOKENS // TOK)
    expert_ids = jax.vmap(lambda own, number: assign_block(jax.random.fold_in(key_of[6], 2), own, number, TOK, EXPERTS, TOPK, CAP, 2))(expert_ids_keys, expert_ids_turns).reshape((TOKENS, TOPK))
    gate_weights = jnp.clip(jnp.exp(math.log(1.0) - 2.3025851 * jax.random.uniform(key_of[7], (TOKENS, TOPK), jnp.float32) ** levels(key_of[7], (TOKENS, TOPK), ((0, 16),), -0.2, 0.2)), 0.1, 1.0)
    grad_out = bell_draw(key_of[8], (TOKENS, D), 1.0, 6.0, ((0, 16), (1, 2)))
    return {"attn_parts": attn_parts, "resid": resid, "norm_gain": norm_gain, "w_gate": w_gate, "w_up": w_up, "w_down": w_down, "expert_ids": expert_ids, "gate_weights": gate_weights, "grad_out": grad_out}


epsilon = 1e-06

def route_tables(expert_ids, gate_weights, experts, capacity):
    pairs = expert_ids.reshape(-1).astype(jnp.int32)
    pair_count = pairs.shape[0]
    expert_hot = (pairs[:, None] == jnp.arange(experts, dtype=jnp.int32)[None, :]).astype(jnp.int32)
    earlier = jnp.cumsum(expert_hot, axis=0) - expert_hot
    position = lax.optimization_barrier(jnp.sum(earlier * expert_hot, axis=1)).astype(jnp.int32)
    slot_index = pairs * capacity + position
    slot_hot = (slot_index[:, None] == jnp.arange(experts * capacity, dtype=jnp.int32)[None, :]).astype(jnp.float32)
    owner = jnp.arange(pair_count, dtype=jnp.int32) // expert_ids.shape[1]
    token_hot = (owner[:, None] == jnp.arange(expert_ids.shape[0], dtype=jnp.int32)[None, :]).astype(jnp.float32)
    dispatch = jnp.dot(slot_hot.T, token_hot, precision=lax.Precision.HIGHEST)
    combine = jnp.dot(token_hot.T, slot_hot * gate_weights.reshape(-1)[:, None], precision=lax.Precision.HIGHEST)
    return (dispatch, combine)

def sliced_product(left, right):
    column_width = left.shape[1] // N_TENSOR
    summed = jnp.zeros((left.shape[0], right.shape[1]), jnp.float32)
    for piece_index in range(N_TENSOR):
        lower = piece_index * column_width
        partial_term = jnp.dot(left[:, lower:lower + column_width], right[lower:lower + column_width], preferred_element_type=jnp.float32)
        summed = summed + lax.optimization_barrier(partial_term.astype(jnp.bfloat16)).astype(jnp.float32)
    return summed

def expert_pass(operands):
    rows, grad_rows_in, gate_matrix, up_matrix, down_matrix = operands
    gate_pre = sliced_product(rows, gate_matrix)
    up_pre = sliced_product(rows, up_matrix)
    activation = (jax.nn.silu(gate_pre) * up_pre).astype(jnp.bfloat16)
    expert_out = jnp.dot(activation, down_matrix, preferred_element_type=jnp.float32).astype(jnp.bfloat16)
    grad_act = sliced_product(grad_rows_in, down_matrix.T)
    sigmoid_gate = jax.nn.sigmoid(gate_pre)
    grad_gate = (grad_act * up_pre * sigmoid_gate * (1.0 + gate_pre * (1.0 - sigmoid_gate))).astype(jnp.bfloat16)
    grad_up = (grad_act * jax.nn.silu(gate_pre)).astype(jnp.bfloat16)
    grad_expert = (jnp.dot(grad_gate, gate_matrix.T, preferred_element_type=jnp.float32) + jnp.dot(grad_up, up_matrix.T, preferred_element_type=jnp.float32)).astype(jnp.bfloat16)
    return (expert_out, grad_expert)

def reference(attn_parts, resid, norm_gain, w_gate, w_up, w_down, expert_ids, gate_weights, grad_out):
    attention = lax.optimization_barrier(jnp.sum(attn_parts.astype(jnp.float32), axis=0))
    hidden_in = resid.astype(jnp.float32) + attention
    inv_rms = lax.rsqrt(lax.optimization_barrier(jnp.sum(hidden_in * hidden_in, axis=1)) / D + epsilon)
    normed = (hidden_in * inv_rms[:, None] * norm_gain[None, :]).astype(jnp.bfloat16)
    upstream = grad_out.astype(jnp.float32)
    groups = TOKENS // TOK

    def group_send(operands):
        group_ids, group_gates, normed_group, upstream_group = operands
        dispatch, combine = route_tables(group_ids, group_gates, EXPERTS, CAP)
        sent = jnp.dot(dispatch.astype(jnp.bfloat16), normed_group, preferred_element_type=jnp.float32).astype(jnp.bfloat16)
        grad_slots = jnp.dot(combine.T, upstream_group, precision=lax.Precision.HIGHEST).astype(jnp.bfloat16)
        return (sent, grad_slots, dispatch, combine)
    sent, grad_slots, dispatch, combine = lax.map(group_send, (expert_ids.reshape(groups, TOK, TOPK), gate_weights.reshape(groups, TOK, TOPK), normed.reshape(groups, TOK, D), upstream.reshape(groups, TOK, D)))

    def to_experts(blocks):
        return blocks.reshape(groups, EXPERTS, CAP, D).transpose(1, 0, 2, 3).reshape(EXPERTS, groups * CAP, D)

    def to_groups(blocks):
        return blocks.reshape(EXPERTS, groups, CAP, D).transpose(1, 0, 2, 3).reshape(groups, EXPERTS * CAP, D)
    expert_out, grad_expert = lax.map(expert_pass, (to_experts(sent), to_experts(grad_slots), w_gate, w_up, w_down))

    def group_gather(operands):
        dispatch_group, combine_group, returned, grad_back = operands
        moe_group = jnp.dot(combine_group, returned.astype(jnp.float32), precision=lax.Precision.HIGHEST)
        grad_group = jnp.dot(dispatch_group.astype(jnp.bfloat16).T, grad_back, preferred_element_type=jnp.float32)
        return (moe_group, grad_group)
    moe, grad_normed = lax.map(group_gather, (dispatch, combine, to_groups(expert_out), to_groups(grad_expert)))
    moe = moe.reshape(TOKENS, D)
    grad_normed = grad_normed.reshape(TOKENS, D)
    output = (hidden_in + moe).astype(jnp.bfloat16)
    scaled = grad_normed * norm_gain[None, :]
    inner = lax.optimization_barrier(jnp.sum(hidden_in * scaled, axis=1))
    grad_input = upstream + inv_rms[:, None] * scaled - hidden_in * (inv_rms ** 3 * inner / D)[:, None]
    return (output, grad_input.astype(jnp.bfloat16))
```

```python
import functools

import jax
import jax.numpy as jnp
from jax import lax
from jax.experimental import pallas as pl
from jax.experimental.pallas import tpu as pltpu
from jax.sharding import PartitionSpec as P

D = 4096
Z = 4
MESH = pl.DeviceIdType.MESH
COLUMNS = 512

epsilon = 1e-06


def device(expert):
    return (expert, lax.axis_index("tensor"))


def position(plane):
    me = lax.axis_index("expert")
    return me, me // plane, me % plane


def greet(plane):
    me, z, p = position(plane)
    barrier = pltpu.get_barrier_semaphore()

    def hello(d, carry):
        pl.semaphore_signal(
            barrier, inc=1, device_id=device(z * plane + (p + d) % plane), device_id_type=MESH
        )
        return carry

    lax.fori_loop(1, plane, hello, 0)

    @pl.when(z > 0)
    def _():
        pl.semaphore_signal(barrier, inc=1, device_id=device(me - plane), device_id_type=MESH)

    @pl.when(z < Z - 1)
    def _():
        pl.semaphore_signal(barrier, inc=1, device_id=device(me + plane), device_id_type=MESH)

    neighbours = (z + Z - 1) // Z + (2 * Z - 2 - z) // Z
    pl.semaphore_wait(barrier, plane - 1 + neighbours)


def dispatch_kernel(
    plane, grad_ref, normed_ref, hot_ref, rows_ref, held, stage, line_send, line_recv, send, recv
):
    me, z, p = position(plane)
    cap, width = stage.shape[3], stage.shape[4]
    sources = (grad_ref, normed_ref)

    def line_copy(a, way, step, source, origin):
        return pltpu.make_async_remote_copy(
            src_ref=source,
            dst_ref=held.at[a, origin],
            send_sem=line_send.at[a, way, step],
            recv_sem=line_recv.at[a, way, step],
            device_id=device(me + plane if way == 0 else me - plane),
            device_id_type=MESH,
        )

    def plane_copy(a, origin, q, sender, target):
        return pltpu.make_async_remote_copy(
            src_ref=stage.at[a, origin, q],
            dst_ref=rows_ref.at[a, origin * plane + sender],
            send_sem=send.at[a, origin, q],
            recv_sem=recv.at[a, origin, sender],
            device_id=device(z * plane + target),
            device_id_type=MESH,
        )

    def spread(a, origin, block):
        hot = hot_ref[origin].reshape(plane * cap, -1)

        def chunk(c, carry):
            columns = pl.ds(pl.multiple_of(c * COLUMNS, COLUMNS), COLUMNS)
            picked = jnp.dot(hot, block[:, columns], preferred_element_type=jnp.float32)
            stage[a, origin, :, :, columns] = picked.astype(jnp.bfloat16).reshape(
                plane, cap, COLUMNS
            )
            return carry

        lax.fori_loop(0, width // COLUMNS, chunk, 0)

        def post(d, carry):
            q = (p + d) % plane
            plane_copy(a, origin, q, p, q).start()
            return carry

        lax.fori_loop(1, plane, post, 0)
        rows_ref[a, origin * plane + p] = stage[a, origin, p]

    greet(plane)
    can_go = (z < Z - 1, z > 0)
    for a in range(2):
        for way in range(2):

            @pl.when(can_go[way])
            def _(a=a, way=way):
                line_copy(a, way, 0, sources[a], z).start()

    for a in range(2):
        spread(a, z, sources[a])
    for step in range(1, Z):
        for a in range(2):
            for way in range(2):
                origin = z - step if way == 0 else z + step
                there = z >= step if way == 0 else z + step < Z

                @pl.when(there)
                def _(a=a, way=way, step=step, origin=origin):
                    line_copy(a, way, step - 1, held.at[a, origin], origin).wait_recv()
                    if step < Z - 1:

                        @pl.when(can_go[way])
                        def _():
                            line_copy(a, way, step, held.at[a, origin], origin).start()

                    spread(a, origin, held.at[a, origin])

    for a in range(2):
        for way in range(2):
            for step in range(Z - 1):
                origin = z - step if way == 0 else z + step
                there = z >= step if way == 0 else z + step < Z

                @pl.when(there & can_go[way])
                def _(a=a, way=way, step=step, origin=origin):
                    line_copy(a, way, step, held.at[a, origin], origin).wait_send()

    def finish(i, carry):
        a, origin, d = i // (Z * plane), (i // plane) % Z, i % plane

        @pl.when(d > 0)
        def _():
            q = (p + d) % plane
            plane_copy(a, origin, q, p, q).wait_send()
            plane_copy(a, origin, q, q, q).wait_recv()

        return carry

    lax.fori_loop(0, 2 * Z * plane, finish, 0)


def combine_kernel(
    plane, out_rows, hot_ref, sum_ref, back, inc, leave, line_send, line_recv, send, recv
):
    me, z, p = position(plane)
    cap, width = back.shape[3], back.shape[4]

    def plane_copy(a, origin, q, sender):
        return pltpu.make_async_remote_copy(
            src_ref=out_rows.at[a, origin * plane + q],
            dst_ref=back.at[a, origin, sender],
            send_sem=send.at[a, origin, q],
            recv_sem=recv.at[a, origin, sender],
            device_id=device(z * plane + q),
            device_id_type=MESH,
        )

    def line_copy(a, way, origin):
        return pltpu.make_async_remote_copy(
            src_ref=leave.at[a, origin],
            dst_ref=inc.at[a, way, origin],
            send_sem=line_send.at[a, origin],
            recv_sem=line_recv.at[a, way, origin],
            device_id=device(me + plane if way == 0 else me - plane),
            device_id_type=MESH,
        )

    def post(a, origin):
        def one(d, carry):
            plane_copy(a, origin, (p + d) % plane, p).start()
            return carry

        lax.fori_loop(1, plane, one, 0)

    def gather(a, origin):
        back[a, origin, p] = out_rows[a, origin * plane + p]

        def one(d, carry):
            q = (p + d) % plane
            plane_copy(a, origin, q, q).wait_recv()
            return carry

        lax.fori_loop(1, plane, one, 0)

    def each_chunk(body):
        def chunk(c, carry):
            body(pl.ds(pl.multiple_of(c * COLUMNS, COLUMNS), COLUMNS))
            return carry

        lax.fori_loop(0, width // COLUMNS, chunk, 0)

    def partial(a, origin, columns):
        rows = back[a, origin, :, :, columns].reshape(plane * cap, COLUMNS)
        return jnp.dot(hot_ref[origin], rows, preferred_element_type=jnp.float32)

    greet(plane)
    comes = (z > 0, z < Z - 1)

    def far(way, step):
        origin = z + step if way == 0 else z - step
        return origin, (z + step < Z if way == 0 else z >= step)

    for step in range(Z - 1, 0, -1):
        for a in range(2):
            for way in range(2):
                origin, there = far(way, step)

                @pl.when(there)
                def _(a=a, origin=origin):
                    post(a, origin)

    for a in range(2):
        post(a, z)

    for step in range(Z - 1, 0, -1):
        for a in range(2):
            for way in range(2):
                origin, there = far(way, step)

                @pl.when(there)
                def _(a=a, way=way, step=step, origin=origin):
                    gather(a, origin)
                    if step == Z - 1:

                        @each_chunk
                        def _(columns):
                            leave[a, origin, :, columns] = partial(a, origin, columns).astype(
                                jnp.bfloat16
                            )
                    else:

                        @pl.when(comes[way])
                        def _():
                            line_copy(a, way, origin).wait_recv()

                            @each_chunk
                            def _(columns):
                                earlier = inc[a, way, origin, :, columns].astype(jnp.float32)
                                leave[a, origin, :, columns] = (
                                    partial(a, origin, columns) + earlier
                                ).astype(jnp.bfloat16)

                        @pl.when(jnp.logical_not(comes[way]))
                        def _():
                            @each_chunk
                            def _(columns):
                                leave[a, origin, :, columns] = partial(a, origin, columns).astype(
                                    jnp.bfloat16
                                )

                    line_copy(a, way, origin).start()

    for a in range(2):
        gather(a, z)

        @each_chunk
        def _(columns, a=a):
            sum_ref[a, :, columns] = partial(a, z, columns)

    for a in range(2):
        for way in range(2):

            @pl.when(comes[way])
            def _(a=a, way=way):
                line_copy(a, way, z).wait_recv()

                @each_chunk
                def _(columns):
                    sum_ref[a, :, columns] += inc[a, way, z, :, columns].astype(jnp.float32)

    for step in range(Z - 1, 0, -1):
        for a in range(2):
            for way in range(2):
                origin, there = far(way, step)

                @pl.when(there)
                def _(a=a, way=way, origin=origin):
                    line_copy(a, way, origin).wait_send()

    def finish(i, carry):
        a, origin, d = i // (Z * plane), (i // plane) % Z, i % plane

        @pl.when(d > 0)
        def _():
            plane_copy(a, origin, (p + d) % plane, p).wait_send()

        return carry

    lax.fori_loop(0, 2 * Z * plane, finish, 0)


VM = pl.BlockSpec(memory_space=pltpu.VMEM)


def dispatch(grad_out, normed, hot, plane, cap):
    tokens, width = normed.shape
    return pl.pallas_call(
        functools.partial(dispatch_kernel, plane),
        out_shape=jax.ShapeDtypeStruct((2, Z * plane, cap, width), jnp.bfloat16),
        in_specs=[VM] * 3,
        out_specs=VM,
        scratch_shapes=[
            pltpu.VMEM((2, Z, tokens, width), jnp.bfloat16),
            pltpu.VMEM((2, Z, plane, cap, width), jnp.bfloat16),
            pltpu.SemaphoreType.DMA((2, 2, Z - 1)),
            pltpu.SemaphoreType.DMA((2, 2, Z - 1)),
            pltpu.SemaphoreType.DMA((2, Z, plane)),
            pltpu.SemaphoreType.DMA((2, Z, plane)),
        ],
        compiler_params=pltpu.CompilerParams(
            collective_id=0, has_side_effects=True, vmem_limit_bytes=48 << 20
        ),
    )(grad_out, normed, hot)


def combine(out_rows, hot, tokens, plane):
    _, _, cap, width = out_rows.shape
    return pl.pallas_call(
        functools.partial(combine_kernel, plane),
        out_shape=jax.ShapeDtypeStruct((2, tokens, width), jnp.float32),
        in_specs=[VM] * 2,
        out_specs=VM,
        scratch_shapes=[
            pltpu.VMEM((2, Z, plane, cap, width), jnp.bfloat16),
            pltpu.VMEM((2, 2, Z, tokens, width), jnp.bfloat16),
            pltpu.VMEM((2, Z, tokens, width), jnp.bfloat16),
            pltpu.SemaphoreType.DMA((2, Z)),
            pltpu.SemaphoreType.DMA((2, 2, Z)),
            pltpu.SemaphoreType.DMA((2, Z, plane)),
            pltpu.SemaphoreType.DMA((2, Z, plane)),
        ],
        compiler_params=pltpu.CompilerParams(
            collective_id=1, has_side_effects=True, vmem_limit_bytes=48 << 20
        ),
    )(out_rows, hot)


def places(named):
    tokens = named.shape[-1]
    order = jnp.arange(tokens, dtype=jnp.int32)
    before = (order[:, None] < order[None, :]).astype(jnp.bfloat16)
    return jnp.dot(
        named.astype(jnp.bfloat16), before, preferred_element_type=jnp.float32
    ).astype(jnp.int32)


def row_sums(values):
    return lax.psum(jnp.sum(values, axis=1), "tensor")


def body(attn_parts, resid, norm_gain, w_gate, w_up, w_down, expert_ids, gate_weights, grad_out):
    experts = lax.axis_size("expert")
    plane = experts // Z
    tokens = expert_ids.shape[0]
    capacity = 5 * tokens * expert_ids.shape[1] // (4 * experts)
    cap = -(-capacity // 16) * 16
    width = resid.shape[1]
    me = lax.axis_index("expert")
    z, p = me // plane, me % plane

    table = lax.all_gather(
        jnp.concatenate([expert_ids.T.astype(jnp.float32), gate_weights.T], axis=0), "expert"
    )
    topk = expert_ids.shape[1]
    ids, gates = table[:, :topk].astype(jnp.int32), table[:, topk:]
    slots = jnp.arange(cap, dtype=jnp.int32)
    line_ids = lax.dynamic_index_in_dim(
        ids.reshape(Z, plane, topk, tokens), p, axis=1, keepdims=False
    )
    plane_experts = z * plane + jnp.arange(plane, dtype=jnp.int32)
    named = jnp.any(line_ids[:, None] == plane_experts[None, :, None, None], axis=2)
    hot = (
        named[:, :, None, :] & (places(named)[:, :, None, :] == slots[None, None, :, None])
    ).astype(jnp.bfloat16)
    hot_back = hot.reshape(Z, plane * cap, tokens).transpose(0, 2, 1)
    here = ids == me
    taken = jnp.any(here, axis=1)
    gate_here = jnp.sum(jnp.where(here, gates, 0.0), axis=1)
    row_gate = jnp.sum(
        jnp.where(
            taken[:, None, :] & (places(taken)[:, None, :] == slots[None, :, None]),
            gate_here[:, None, :],
            0.0,
        ),
        axis=2,
    ).reshape(experts * cap, 1)

    attention = lax.psum_scatter(
        attn_parts[0], "tensor", scatter_dimension=1, tiled=True
    ).astype(jnp.float32)
    hidden_in = resid.astype(jnp.float32) + attention
    inv_rms = lax.rsqrt(row_sums(hidden_in * hidden_in) / D + epsilon)
    normed = (hidden_in * inv_rms[:, None] * norm_gain[None, :]).astype(jnp.bfloat16)

    arrived = dispatch(grad_out, normed, hot, plane, cap).reshape(2, experts * cap, width)
    grad_rows, rows = arrived[0], arrived[1]
    gate_part = jnp.dot(rows, w_gate[0], preferred_element_type=jnp.float32)
    up_part = jnp.dot(rows, w_up[0], preferred_element_type=jnp.float32)
    grad_part = jnp.dot(grad_rows, w_down[0].T, preferred_element_type=jnp.float32)
    summed = lax.psum(
        jnp.stack([gate_part, up_part, grad_part]).astype(jnp.bfloat16), "tensor"
    ).astype(jnp.float32)
    gate_pre, up_pre, grad_act = summed[0], summed[1], summed[2] * row_gate
    sigmoid_gate = jax.nn.sigmoid(gate_pre)
    swish = gate_pre * sigmoid_gate
    activation = (swish * up_pre).astype(jnp.bfloat16)
    expert_out = (
        jnp.dot(activation, w_down[0], preferred_element_type=jnp.float32) * row_gate
    ).astype(jnp.bfloat16)
    grad_gate = grad_act * up_pre * sigmoid_gate * (1.0 + gate_pre * (1.0 - sigmoid_gate))
    grad_up = grad_act * swish
    grad_expert = (
        jnp.dot(grad_gate.astype(jnp.bfloat16), w_gate[0].T, preferred_element_type=jnp.float32)
        + jnp.dot(grad_up.astype(jnp.bfloat16), w_up[0].T, preferred_element_type=jnp.float32)
    ).astype(jnp.bfloat16)
    out_rows = jnp.stack([expert_out, grad_expert]).reshape(2, experts, cap, width)
    sums = combine(out_rows, hot_back, tokens, plane)
    moe, grad_normed = sums[0], sums[1]

    output = (hidden_in + moe).astype(jnp.bfloat16)
    scaled = grad_normed * norm_gain[None, :]
    inner = row_sums(hidden_in * scaled)
    grad_input = (
        grad_out.astype(jnp.float32)
        + inv_rms[:, None] * scaled
        - hidden_in * (inv_rms**3 * inner / D)[:, None]
    )
    return (output, grad_input.astype(jnp.bfloat16))


def solution(mesh):
    return jax.shard_map(
        body,
        mesh=mesh,
        in_specs=(
            P("tensor", "expert", None),
            P("expert", "tensor"),
            P("tensor"),
            P("expert", "tensor", None),
            P("expert", "tensor", None),
            P("expert", None, "tensor"),
            P("expert", None),
            P("expert", None),
            P("expert", "tensor"),
        ),
        out_specs=(P("expert", "tensor"), P("expert", "tensor")),
        check_vma=False,
    )
```

```python
import functools

import jax
import jax.numpy as jnp
from jax import lax
from jax.experimental import pallas as pl
from jax.experimental.pallas import tpu as pltpu
from jax.sharding import PartitionSpec as P

D = 4096
Z = 4
MESH = pl.DeviceIdType.MESH
COLUMNS = 512

epsilon = 1e-06


def device(expert):
    return (expert, lax.axis_index("tensor"))


def position(plane):
    me = lax.axis_index("expert")
    return me, me // plane, me % plane


def partner():
    return (lax.axis_index("expert"), 1 - lax.axis_index("tensor"))


def greet(plane, pair):
    me, z, p = position(plane)
    barrier = pltpu.get_barrier_semaphore()
    if pair:
        pl.semaphore_signal(barrier, inc=1, device_id=partner(), device_id_type=MESH)

    def hello(d, carry):
        pl.semaphore_signal(
            barrier, inc=1, device_id=device(z * plane + (p + d) % plane), device_id_type=MESH
        )
        return carry

    lax.fori_loop(1, plane, hello, 0)

    @pl.when(z > 0)
    def _():
        pl.semaphore_signal(barrier, inc=1, device_id=device(me - plane), device_id_type=MESH)

    @pl.when(z < Z - 1)
    def _():
        pl.semaphore_signal(barrier, inc=1, device_id=device(me + plane), device_id_type=MESH)

    neighbours = (z + Z - 1) // Z + (2 * Z - 2 - z) // Z
    pl.semaphore_wait(barrier, plane - 1 + int(pair) + neighbours)


def dispatch_kernel(
    plane,
    attn_ref,
    resid_ref,
    gain_ref,
    grad_ref,
    table_ref,
    rows_ref,
    hidden_ref,
    inv_ref,
    hot_ref,
    gate_ref,
    held,
    stage,
    normed,
    other,
    stat,
    tables,
    line_send,
    line_recv,
    send,
    recv,
    table_send,
    table_recv,
    pair_send,
    pair_recv,
):
    me, z, p = position(plane)
    cap, width = stage.shape[3], stage.shape[4]
    tokens = table_ref.shape[1]
    topk = table_ref.shape[0] // 2
    side = lax.axis_index("tensor")
    sources = (grad_ref, normed)

    def pair_copy(i, source, target):
        return pltpu.make_async_remote_copy(
            src_ref=source,
            dst_ref=target,
            send_sem=pair_send.at[i],
            recv_sem=pair_recv.at[i],
            device_id=partner(),
            device_id_type=MESH,
        )

    def half(of):
        return pl.ds(pl.multiple_of(of * width, width), width)

    attn_copy = pair_copy(0, attn_ref.at[:, half(1 - side)], other)
    stat_copy = pair_copy(1, stat.at[0], stat.at[1])

    def table_copy(way, step, source, origin):
        return pltpu.make_async_remote_copy(
            src_ref=source,
            dst_ref=tables.at[origin],
            send_sem=table_send.at[way, step],
            recv_sem=table_recv.at[way, step],
            device_id=device(me + plane if way == 0 else me - plane),
            device_id_type=MESH,
        )

    def find_slots(origin, table):
        count = max(16, plane)
        expert = (z * plane + lax.broadcasted_iota(jnp.int32, (count, tokens), 0)).astype(
            jnp.float32
        )
        named = jnp.zeros((count, tokens), jnp.float32)
        gates = jnp.zeros((count, tokens), jnp.float32)
        for k in range(topk):
            hit = table[k : k + 1, :] == expert
            named = jnp.where(hit, 1.0, named)
            gates = jnp.where(hit, table[topk + k : topk + k + 1, :], gates)
        before = jnp.where(
            lax.broadcasted_iota(jnp.int32, (tokens, tokens), 0)
            < lax.broadcasted_iota(jnp.int32, (tokens, tokens), 1),
            1.0,
            0.0,
        ).astype(jnp.bfloat16)
        earlier = jnp.dot(named.astype(jnp.bfloat16), before, preferred_element_type=jnp.float32)
        slot = jnp.where(named > 0.5, earlier, -1.0)
        number = lax.broadcasted_iota(jnp.int32, (cap, tokens), 0).astype(jnp.float32)
        for e in range(plane):
            own = slot[e : e + 1, :] == number
            hot_ref[origin, e * cap : (e + 1) * cap, :] = jnp.where(own, 1.0, 0.0).astype(
                jnp.bfloat16
            )
            weight = jnp.sum(jnp.where(own, gates[e : e + 1, :], 0.0), axis=1, keepdims=True)
            gate_ref[origin, e * cap : (e + 1) * cap, :] = jnp.broadcast_to(weight, (cap, tokens))

    def each_chunk(body):
        def chunk(c, carry):
            body(pl.ds(pl.multiple_of(c * COLUMNS, COLUMNS), COLUMNS))
            return carry

        lax.fori_loop(0, width // COLUMNS, chunk, 0)

    def norm():
        stat[0] = jnp.zeros((tokens, 128), jnp.float32)
        attn_copy.wait_recv()

        def chunk(c, carry):
            columns = pl.ds(pl.multiple_of(c * COLUMNS, COLUMNS), COLUMNS)
            own = pl.ds(pl.multiple_of(side * width + c * COLUMNS, COLUMNS), COLUMNS)
            value = resid_ref[:, columns].astype(jnp.float32) + (
                attn_ref[:, own].astype(jnp.float32) + other[:, columns].astype(jnp.float32)
            )
            hidden_ref[:, columns] = value
            squares = jnp.sum(value * value, axis=1, keepdims=True)
            stat[0] += jnp.broadcast_to(squares, (tokens, 128))
            return carry

        lax.fori_loop(0, width // COLUMNS, chunk, 0)
        stat_copy.start()
        stat_copy.wait_recv()
        inv_ref[...] = lax.rsqrt((stat[0] + stat[1]) / D + epsilon)

        @each_chunk
        def _(columns):
            normed[:, columns] = (
                hidden_ref[:, columns] * inv_ref[:, 0:1] * gain_ref[:, columns]
            ).astype(jnp.bfloat16)

    def line_copy(a, way, step, source, origin):
        return pltpu.make_async_remote_copy(
            src_ref=source,
            dst_ref=held.at[a, origin],
            send_sem=line_send.at[a, way, step],
            recv_sem=line_recv.at[a, way, step],
            device_id=device(me + plane if way == 0 else me - plane),
            device_id_type=MESH,
        )

    def plane_copy(a, origin, q, sender, target):
        return pltpu.make_async_remote_copy(
            src_ref=stage.at[a, origin, q],
            dst_ref=rows_ref.at[a, origin * plane + sender],
            send_sem=send.at[a, origin, q],
            recv_sem=recv.at[a, origin, sender],
            device_id=device(z * plane + target),
            device_id_type=MESH,
        )

    def spread(a, origin, block):
        @each_chunk
        def _(columns):
            picked = jnp.dot(
                hot_ref[origin], block[:, columns], preferred_element_type=jnp.float32
            )
            if a == 0:
                picked = picked * gate_ref[origin, :, 0:1]
            stage[a, origin, :, :, columns] = picked.astype(jnp.bfloat16).reshape(
                plane, cap, COLUMNS
            )

        def post(d, carry):
            q = (p + d) % plane
            plane_copy(a, origin, q, p, q).start()
            return carry

        lax.fori_loop(1, plane, post, 0)
        rows_ref[a, origin * plane + p] = stage[a, origin, p]

    greet(plane, True)
    can_go = (z < Z - 1, z > 0)
    attn_copy.start()

    def set_out(a):
        for way in range(2):

            @pl.when(can_go[way])
            def _(way=way):
                if a == 0:
                    table_copy(way, 0, table_ref, z).start()
                line_copy(a, way, 0, sources[a], z).start()

    set_out(0)
    find_slots(z, table_ref[...])
    spread(0, z, grad_ref)
    norm()
    set_out(1)
    spread(1, z, normed)
    for step in range(1, Z):
        for a in range(2):
            for way in range(2):
                origin = z - step if way == 0 else z + step
                there = z >= step if way == 0 else z + step < Z

                @pl.when(there)
                def _(a=a, way=way, step=step, origin=origin):
                    if a == 0:
                        table_copy(way, step - 1, tables.at[origin], origin).wait_recv()
                        if step < Z - 1:

                            @pl.when(can_go[way])
                            def _():
                                table_copy(way, step, tables.at[origin], origin).start()

                    line_copy(a, way, step - 1, held.at[a, origin], origin).wait_recv()
                    if step < Z - 1:

                        @pl.when(can_go[way])
                        def _():
                            line_copy(a, way, step, held.at[a, origin], origin).start()

                    if a == 0:
                        find_slots(origin, tables[origin])
                    spread(a, origin, held.at[a, origin])

    for a in range(2):
        for way in range(2):
            for step in range(Z - 1):
                origin = z - step if way == 0 else z + step
                there = z >= step if way == 0 else z + step < Z

                @pl.when(there & can_go[way])
                def _(a=a, way=way, step=step, origin=origin):
                    if a == 0:
                        table_copy(way, step, tables.at[origin], origin).wait_send()
                    line_copy(a, way, step, held.at[a, origin], origin).wait_send()

    attn_copy.wait_send()
    stat_copy.wait_send()

    def finish(i, carry):
        a, origin, d = i // (Z * plane), (i // plane) % Z, i % plane

        @pl.when(d > 0)
        def _():
            q = (p + d) % plane
            plane_copy(a, origin, q, p, q).wait_send()
            plane_copy(a, origin, q, q, q).wait_recv()

        return carry

    lax.fori_loop(0, 2 * Z * plane, finish, 0)


def combine_kernel(
    plane, out_rows, hot_ref, gate_ref, sum_ref, back, inc, leave, line_send, line_recv, send, recv
):
    me, z, p = position(plane)
    cap, width = back.shape[3], back.shape[4]

    def plane_copy(a, origin, q, sender):
        return pltpu.make_async_remote_copy(
            src_ref=out_rows.at[a, origin * plane + q],
            dst_ref=back.at[a, origin, sender],
            send_sem=send.at[a, origin, q],
            recv_sem=recv.at[a, origin, sender],
            device_id=device(z * plane + q),
            device_id_type=MESH,
        )

    def line_copy(a, way, origin):
        return pltpu.make_async_remote_copy(
            src_ref=leave.at[a, origin],
            dst_ref=inc.at[a, way, origin],
            send_sem=line_send.at[a, origin],
            recv_sem=line_recv.at[a, way, origin],
            device_id=device(me + plane if way == 0 else me - plane),
            device_id_type=MESH,
        )

    def post(a, origin):
        def one(d, carry):
            plane_copy(a, origin, (p + d) % plane, p).start()
            return carry

        lax.fori_loop(1, plane, one, 0)

    def gather(a, origin):
        back[a, origin, p] = out_rows[a, origin * plane + p]

        def one(d, carry):
            q = (p + d) % plane
            plane_copy(a, origin, q, q).wait_recv()
            return carry

        lax.fori_loop(1, plane, one, 0)

    def each_chunk(body):
        def chunk(c, carry):
            body(pl.ds(pl.multiple_of(c * COLUMNS, COLUMNS), COLUMNS))
            return carry

        lax.fori_loop(0, width // COLUMNS, chunk, 0)

    def partial(a, origin, columns):
        rows = back[a, origin, :, :, columns].reshape(plane * cap, COLUMNS)
        first = (((0,), (0,)), ((), ()))
        hot = hot_ref[origin]
        if a == 1:
            return lax.dot_general(hot, rows, first, preferred_element_type=jnp.float32)
        weight = hot.astype(jnp.float32) * gate_ref[origin]
        high = weight.astype(jnp.bfloat16)
        low = (weight - high.astype(jnp.float32)).astype(jnp.bfloat16)
        return lax.dot_general(
            high, rows, first, preferred_element_type=jnp.float32
        ) + lax.dot_general(low, rows, first, preferred_element_type=jnp.float32)

    greet(plane, False)
    comes = (z > 0, z < Z - 1)

    def far(way, step):
        origin = z + step if way == 0 else z - step
        return origin, (z + step < Z if way == 0 else z >= step)

    for step in range(Z - 1, 0, -1):
        for a in range(2):
            for way in range(2):
                origin, there = far(way, step)

                @pl.when(there)
                def _(a=a, origin=origin):
                    post(a, origin)

    for a in range(2):
        post(a, z)

    for step in range(Z - 1, 0, -1):
        for a in range(2):
            for way in range(2):
                origin, there = far(way, step)

                @pl.when(there)
                def _(a=a, way=way, step=step, origin=origin):
                    gather(a, origin)
                    if step == Z - 1:

                        @each_chunk
                        def _(columns):
                            leave[a, origin, :, columns] = partial(a, origin, columns).astype(
                                jnp.bfloat16
                            )
                    else:

                        @pl.when(comes[way])
                        def _():
                            line_copy(a, way, origin).wait_recv()

                            @each_chunk
                            def _(columns):
                                earlier = inc[a, way, origin, :, columns].astype(jnp.float32)
                                leave[a, origin, :, columns] = (
                                    partial(a, origin, columns) + earlier
                                ).astype(jnp.bfloat16)

                        @pl.when(jnp.logical_not(comes[way]))
                        def _():
                            @each_chunk
                            def _(columns):
                                leave[a, origin, :, columns] = partial(a, origin, columns).astype(
                                    jnp.bfloat16
                                )

                    line_copy(a, way, origin).start()

    for a in range(2):
        gather(a, z)

        @each_chunk
        def _(columns, a=a):
            sum_ref[a, :, columns] = partial(a, z, columns)

    for a in range(2):
        for way in range(2):

            @pl.when(comes[way])
            def _(a=a, way=way):
                line_copy(a, way, z).wait_recv()

                @each_chunk
                def _(columns):
                    sum_ref[a, :, columns] += inc[a, way, z, :, columns].astype(jnp.float32)

    for step in range(Z - 1, 0, -1):
        for a in range(2):
            for way in range(2):
                origin, there = far(way, step)

                @pl.when(there)
                def _(a=a, way=way, origin=origin):
                    line_copy(a, way, origin).wait_send()

    def finish(i, carry):
        a, origin, d = i // (Z * plane), (i // plane) % Z, i % plane

        @pl.when(d > 0)
        def _():
            plane_copy(a, origin, (p + d) % plane, p).wait_send()

        return carry

    lax.fori_loop(0, 2 * Z * plane, finish, 0)


VM = pl.BlockSpec(memory_space=pltpu.VMEM)


def expert_kernel(
    rows_ref, gate_ref, up_ref, down_ref, out_ref, mine, theirs, send, recv
):
    count, part = mine.shape[0], mine.shape[2]
    width = rows_ref.shape[2]
    last = (((1,), (1,)), ((), ()))
    barrier = pltpu.get_barrier_semaphore()
    pl.semaphore_signal(barrier, inc=1, device_id=partner(), device_id_type=MESH)
    pl.semaphore_wait(barrier, 1)

    def copy(c):
        return pltpu.make_async_remote_copy(
            src_ref=mine.at[c],
            dst_ref=theirs.at[c],
            send_sem=send.at[c],
            recv_sem=recv.at[c],
            device_id=partner(),
            device_id_type=MESH,
        )

    def first_half(c, carry):
        at = pl.ds(pl.multiple_of(c * part, part), part)
        rows = rows_ref[1, at, :]
        mine[c, 0] = jnp.dot(rows, gate_ref[...], preferred_element_type=jnp.float32).astype(
            jnp.bfloat16
        )
        mine[c, 1] = jnp.dot(rows, up_ref[...], preferred_element_type=jnp.float32).astype(
            jnp.bfloat16
        )
        mine[c, 2] = lax.dot_general(
            rows_ref[0, at, :], down_ref[...], last, preferred_element_type=jnp.float32
        ).astype(jnp.bfloat16)
        copy(c).start()
        return carry

    def second_half(c, carry):
        at = pl.ds(pl.multiple_of(c * part, part), part)
        copy(c).wait()
        gate_pre, up_pre, grad_act = (
            mine[c, i].astype(jnp.float32) + theirs[c, i].astype(jnp.float32) for i in range(3)
        )
        sigmoid_gate = 1.0 / (1.0 + jnp.exp(-gate_pre))
        swish = gate_pre * sigmoid_gate
        mine[c, 0] = (swish * up_pre).astype(jnp.bfloat16)
        mine[c, 1] = (
            grad_act * up_pre * sigmoid_gate * (1.0 + gate_pre * (1.0 - sigmoid_gate))
        ).astype(jnp.bfloat16)
        mine[c, 2] = (grad_act * swish).astype(jnp.bfloat16)

        def chunk(i, inner):
            columns = pl.ds(pl.multiple_of(i * COLUMNS, COLUMNS), COLUMNS)
            out_ref[0, at, columns] = jnp.dot(
                mine[c, 0], down_ref[:, columns], preferred_element_type=jnp.float32
            ).astype(jnp.bfloat16)
            out_ref[1, at, columns] = (
                lax.dot_general(
                    mine[c, 1], gate_ref[columns, :], last, preferred_element_type=jnp.float32
                )
                + lax.dot_general(
                    mine[c, 2], up_ref[columns, :], last, preferred_element_type=jnp.float32
                )
            ).astype(jnp.bfloat16)
            return inner

        lax.fori_loop(0, width // COLUMNS, chunk, 0)
        return carry

    lax.fori_loop(0, count, first_half, 0)
    lax.fori_loop(0, count, second_half, 0)


def expert_layer(rows, w_gate, w_up, w_down):
    _, total, width = rows.shape
    hidden = w_gate.shape[1]
    part = 256
    count = total // part
    return pl.pallas_call(
        expert_kernel,
        out_shape=jax.ShapeDtypeStruct((2, total, width), jnp.bfloat16),
        in_specs=[VM] * 4,
        out_specs=VM,
        scratch_shapes=[
            pltpu.VMEM((count, 3, part, hidden), jnp.bfloat16),
            pltpu.VMEM((count, 3, part, hidden), jnp.bfloat16),
            pltpu.SemaphoreType.DMA((count,)),
            pltpu.SemaphoreType.DMA((count,)),
        ],
        compiler_params=pltpu.CompilerParams(
            collective_id=2, has_side_effects=True, vmem_limit_bytes=52 << 20
        ),
    )(rows, w_gate, w_up, w_down)


def dispatch(attn, resid, gain, grad_out, table, plane, cap):
    tokens, width = resid.shape
    return pl.pallas_call(
        functools.partial(dispatch_kernel, plane),
        out_shape=(
            jax.ShapeDtypeStruct((2, Z * plane, cap, width), jnp.bfloat16),
            jax.ShapeDtypeStruct((tokens, width), jnp.float32),
            jax.ShapeDtypeStruct((tokens, 128), jnp.float32),
            jax.ShapeDtypeStruct((Z, plane * cap, tokens), jnp.bfloat16),
            jax.ShapeDtypeStruct((Z, plane * cap, tokens), jnp.float32),
        ),
        in_specs=[VM] * 5,
        out_specs=(VM,) * 5,
        scratch_shapes=[
            pltpu.VMEM((2, Z, tokens, width), jnp.bfloat16),
            pltpu.VMEM((2, Z, plane, cap, width), jnp.bfloat16),
            pltpu.VMEM((tokens, width), jnp.bfloat16),
            pltpu.VMEM((tokens, width), jnp.bfloat16),
            pltpu.VMEM((2, tokens, 128), jnp.float32),
            pltpu.VMEM((Z,) + table.shape, jnp.float32),
            pltpu.SemaphoreType.DMA((2, 2, Z - 1)),
            pltpu.SemaphoreType.DMA((2, 2, Z - 1)),
            pltpu.SemaphoreType.DMA((2, Z, plane)),
            pltpu.SemaphoreType.DMA((2, Z, plane)),
            pltpu.SemaphoreType.DMA((2, Z - 1)),
            pltpu.SemaphoreType.DMA((2, Z - 1)),
            pltpu.SemaphoreType.DMA((2,)),
            pltpu.SemaphoreType.DMA((2,)),
        ],
        compiler_params=pltpu.CompilerParams(
            collective_id=0, has_side_effects=True, vmem_limit_bytes=48 << 20
        ),
    )(attn, resid, gain, grad_out, table)


def combine(out_rows, hot, gate, tokens, plane):
    _, _, cap, width = out_rows.shape
    return pl.pallas_call(
        functools.partial(combine_kernel, plane),
        out_shape=jax.ShapeDtypeStruct((2, tokens, width), jnp.float32),
        in_specs=[VM] * 3,
        out_specs=VM,
        scratch_shapes=[
            pltpu.VMEM((2, Z, plane, cap, width), jnp.bfloat16),
            pltpu.VMEM((2, 2, Z, tokens, width), jnp.bfloat16),
            pltpu.VMEM((2, Z, tokens, width), jnp.bfloat16),
            pltpu.SemaphoreType.DMA((2, Z)),
            pltpu.SemaphoreType.DMA((2, 2, Z)),
            pltpu.SemaphoreType.DMA((2, Z, plane)),
            pltpu.SemaphoreType.DMA((2, Z, plane)),
        ],
        compiler_params=pltpu.CompilerParams(
            collective_id=1, has_side_effects=True, vmem_limit_bytes=48 << 20
        ),
    )(out_rows, hot, gate)


def row_sums(values):
    return lax.psum(jnp.sum(values, axis=1), "tensor")


def body(attn_parts, resid, norm_gain, w_gate, w_up, w_down, expert_ids, gate_weights, grad_out):
    experts = lax.axis_size("expert")
    plane = experts // Z
    tokens = expert_ids.shape[0]
    capacity = 5 * tokens * expert_ids.shape[1] // (4 * experts)
    cap = -(-capacity // 16) * 16
    width = resid.shape[1]
    table = jnp.concatenate([expert_ids.T.astype(jnp.float32), gate_weights.T], axis=0)
    rows, hidden_in, inv, hot, gate = dispatch(
        attn_parts[0], resid, norm_gain[None, :], grad_out, table, plane, cap
    )
    inv_rms = inv[:, 0]
    out_rows = expert_layer(
        rows.reshape(2, experts * cap, width), w_gate[0], w_up[0], w_down[0]
    ).reshape(2, experts, cap, width)
    sums = combine(out_rows, hot, gate, tokens, plane)
    moe, grad_normed = sums[0], sums[1]

    output = (hidden_in + moe).astype(jnp.bfloat16)
    scaled = grad_normed * norm_gain[None, :]
    inner = row_sums(hidden_in * scaled)
    grad_input = (
        grad_out.astype(jnp.float32)
        + inv_rms[:, None] * scaled
        - hidden_in * (inv_rms**3 * inner / D)[:, None]
    )
    return (output, grad_input.astype(jnp.bfloat16))


def solution(mesh):
    return jax.shard_map(
        body,
        mesh=mesh,
        in_specs=(
            P("tensor", "expert", None),
            P("expert", "tensor"),
            P("tensor"),
            P("expert", "tensor", None),
            P("expert", "tensor", None),
            P("expert", None, "tensor"),
            P("expert", None),
            P("expert", None),
            P("expert", "tensor"),
        ),
        out_specs=(P("expert", "tensor"), P("expert", "tensor")),
        check_vma=False,
    )
```

```python
import functools

import jax
import jax.numpy as jnp
from jax import lax
from jax.experimental import pallas as pl
from jax.experimental.pallas import tpu as pltpu
from jax.sharding import PartitionSpec as P

D = 4096
Z = 4
MESH = pl.DeviceIdType.MESH
COLUMNS = 512

epsilon = 1e-06


def device(expert):
    return (expert, lax.axis_index("tensor"))


def position(plane):
    me = lax.axis_index("expert")
    return me, me // plane, me % plane


def partner():
    return (lax.axis_index("expert"), 1 - lax.axis_index("tensor"))


def greet(plane, pair):
    me, z, p = position(plane)
    barrier = pltpu.get_barrier_semaphore()
    if pair:
        pl.semaphore_signal(barrier, inc=1, device_id=partner(), device_id_type=MESH)

    def hello(d, carry):
        pl.semaphore_signal(
            barrier, inc=1, device_id=device(z * plane + (p + d) % plane), device_id_type=MESH
        )
        return carry

    lax.fori_loop(1, plane, hello, 0)

    @pl.when(z > 0)
    def _():
        pl.semaphore_signal(barrier, inc=1, device_id=device(me - plane), device_id_type=MESH)

    @pl.when(z < Z - 1)
    def _():
        pl.semaphore_signal(barrier, inc=1, device_id=device(me + plane), device_id_type=MESH)

    neighbours = (z + Z - 1) // Z + (2 * Z - 2 - z) // Z
    pl.semaphore_wait(barrier, plane - 1 + int(pair) + neighbours)


def dispatch_kernel(
    plane,
    attn_ref,
    resid_ref,
    gain_ref,
    grad_ref,
    table_ref,
    rows_ref,
    hidden_ref,
    inv_ref,
    hot_ref,
    gate_ref,
    held,
    stage,
    normed,
    other,
    stat,
    tables,
    line_send,
    line_recv,
    send,
    recv,
    table_send,
    table_recv,
    pair_send,
    pair_recv,
):
    me, z, p = position(plane)
    cap, width = stage.shape[3], stage.shape[4]
    tokens = table_ref.shape[1]
    topk = table_ref.shape[0] // 2
    side = lax.axis_index("tensor")
    sources = (grad_ref, normed)

    def pair_copy(i, source, target):
        return pltpu.make_async_remote_copy(
            src_ref=source,
            dst_ref=target,
            send_sem=pair_send.at[i],
            recv_sem=pair_recv.at[i],
            device_id=partner(),
            device_id_type=MESH,
        )

    def half(of):
        return pl.ds(pl.multiple_of(of * width, width), width)

    attn_copy = pair_copy(0, attn_ref.at[:, half(1 - side)], other)
    stat_copy = pair_copy(1, stat.at[0], stat.at[1])

    def table_copy(way, step, source, origin):
        return pltpu.make_async_remote_copy(
            src_ref=source,
            dst_ref=tables.at[origin],
            send_sem=table_send.at[way, step],
            recv_sem=table_recv.at[way, step],
            device_id=device(me + plane if way == 0 else me - plane),
            device_id_type=MESH,
        )

    def find_slots(origin, table):
        count = max(16, plane)
        expert = (z * plane + lax.broadcasted_iota(jnp.int32, (count, tokens), 0)).astype(
            jnp.float32
        )
        named = jnp.zeros((count, tokens), jnp.float32)
        gates = jnp.zeros((count, tokens), jnp.float32)
        for k in range(topk):
            hit = table[k : k + 1, :] == expert
            named = jnp.where(hit, 1.0, named)
            gates = jnp.where(hit, table[topk + k : topk + k + 1, :], gates)
        before = jnp.where(
            lax.broadcasted_iota(jnp.int32, (tokens, tokens), 0)
            < lax.broadcasted_iota(jnp.int32, (tokens, tokens), 1),
            1.0,
            0.0,
        ).astype(jnp.bfloat16)
        earlier = jnp.dot(named.astype(jnp.bfloat16), before, preferred_element_type=jnp.float32)
        slot = jnp.where(named > 0.5, earlier, -1.0)
        number = lax.broadcasted_iota(jnp.int32, (cap, tokens), 0).astype(jnp.float32)
        for e in range(plane):
            own = slot[e : e + 1, :] == number
            hot_ref[origin, e * cap : (e + 1) * cap, :] = jnp.where(own, 1.0, 0.0).astype(
                jnp.bfloat16
            )
            weight = jnp.sum(jnp.where(own, gates[e : e + 1, :], 0.0), axis=1, keepdims=True)
            gate_ref[origin, e * cap : (e + 1) * cap, :] = jnp.broadcast_to(weight, (cap, tokens))

    def each_chunk(body):
        def chunk(c, carry):
            body(pl.ds(pl.multiple_of(c * COLUMNS, COLUMNS), COLUMNS))
            return carry

        lax.fori_loop(0, width // COLUMNS, chunk, 0)

    def norm():
        stat[0] = jnp.zeros((tokens, 128), jnp.float32)
        attn_copy.wait_recv()

        def chunk(c, carry):
            columns = pl.ds(pl.multiple_of(c * COLUMNS, COLUMNS), COLUMNS)
            own = pl.ds(pl.multiple_of(side * width + c * COLUMNS, COLUMNS), COLUMNS)
            value = resid_ref[:, columns].astype(jnp.float32) + (
                attn_ref[:, own].astype(jnp.float32) + other[:, columns].astype(jnp.float32)
            )
            hidden_ref[:, columns] = value
            squares = jnp.sum(value * value, axis=1, keepdims=True)
            stat[0] += jnp.broadcast_to(squares, (tokens, 128))
            return carry

        lax.fori_loop(0, width // COLUMNS, chunk, 0)
        stat_copy.start()
        stat_copy.wait_recv()
        inv_ref[...] = lax.rsqrt((stat[0] + stat[1]) / D + epsilon)

        @each_chunk
        def _(columns):
            normed[:, columns] = (
                hidden_ref[:, columns] * inv_ref[:, 0:1] * gain_ref[:, columns]
            ).astype(jnp.bfloat16)

    def line_copy(a, way, step, source, origin):
        return pltpu.make_async_remote_copy(
            src_ref=source,
            dst_ref=held.at[a, origin],
            send_sem=line_send.at[a, way, step],
            recv_sem=line_recv.at[a, way, step],
            device_id=device(me + plane if way == 0 else me - plane),
            device_id_type=MESH,
        )

    def plane_copy(a, origin, q, sender, target):
        return pltpu.make_async_remote_copy(
            src_ref=stage.at[a, origin, q],
            dst_ref=rows_ref.at[a, origin * plane + sender],
            send_sem=send.at[a, origin, q],
            recv_sem=recv.at[a, origin, sender],
            device_id=device(z * plane + target),
            device_id_type=MESH,
        )

    def spread(a, origin, block):
        @each_chunk
        def _(columns):
            picked = jnp.dot(
                hot_ref[origin], block[:, columns], preferred_element_type=jnp.float32
            )
            if a == 0:
                picked = picked * gate_ref[origin, :, 0:1]
            stage[a, origin, :, :, columns] = picked.astype(jnp.bfloat16).reshape(
                plane, cap, COLUMNS
            )

        def post(d, carry):
            q = (p + d) % plane
            plane_copy(a, origin, q, p, q).start()
            return carry

        lax.fori_loop(1, plane, post, 0)
        rows_ref[a, origin * plane + p] = stage[a, origin, p]

    greet(plane, True)
    can_go = (z < Z - 1, z > 0)
    attn_copy.start()

    def set_out(a):
        for way in range(2):

            @pl.when(can_go[way])
            def _(way=way):
                if a == 0:
                    table_copy(way, 0, table_ref, z).start()
                line_copy(a, way, 0, sources[a], z).start()

    set_out(0)
    find_slots(z, table_ref[...])
    spread(0, z, grad_ref)
    norm()
    set_out(1)
    spread(1, z, normed)
    for step in range(1, Z):
        for a in range(2):
            for way in range(2):
                origin = z - step if way == 0 else z + step
                there = z >= step if way == 0 else z + step < Z

                @pl.when(there)
                def _(a=a, way=way, step=step, origin=origin):
                    if a == 0:
                        table_copy(way, step - 1, tables.at[origin], origin).wait_recv()
                        if step < Z - 1:

                            @pl.when(can_go[way])
                            def _():
                                table_copy(way, step, tables.at[origin], origin).start()

                    line_copy(a, way, step - 1, held.at[a, origin], origin).wait_recv()
                    if step < Z - 1:

                        @pl.when(can_go[way])
                        def _():
                            line_copy(a, way, step, held.at[a, origin], origin).start()

                    if a == 0:
                        find_slots(origin, tables[origin])
                    spread(a, origin, held.at[a, origin])

    for a in range(2):
        for way in range(2):
            for step in range(Z - 1):
                origin = z - step if way == 0 else z + step
                there = z >= step if way == 0 else z + step < Z

                @pl.when(there & can_go[way])
                def _(a=a, way=way, step=step, origin=origin):
                    if a == 0:
                        table_copy(way, step, tables.at[origin], origin).wait_send()
                    line_copy(a, way, step, held.at[a, origin], origin).wait_send()

    attn_copy.wait_send()
    stat_copy.wait_send()

    def finish(i, carry):
        a, origin, d = i // (Z * plane), (i // plane) % Z, i % plane

        @pl.when(d > 0)
        def _():
            q = (p + d) % plane
            plane_copy(a, origin, q, p, q).wait_send()
            plane_copy(a, origin, q, q, q).wait_recv()

        return carry

    lax.fori_loop(0, 2 * Z * plane, finish, 0)


def combine_kernel(
    plane,
    rows_ref,
    w_gate,
    w_up,
    w_down,
    hot_ref,
    gate_ref,
    sum_ref,
    out_rows,
    mine,
    theirs,
    back,
    inc,
    leave,
    line_send,
    line_recv,
    send,
    recv,
    pair_send,
    pair_recv,
):
    me, z, p = position(plane)
    cap, width = back.shape[3], back.shape[4]
    last = (((1,), (1,)), ((), ()))

    def pair_copy(c):
        return pltpu.make_async_remote_copy(
            src_ref=mine.at[c],
            dst_ref=theirs.at[c],
            send_sem=pair_send.at[c],
            recv_sem=pair_recv.at[c],
            device_id=partner(),
            device_id_type=MESH,
        )

    def first_half(c):
        rows = rows_ref[1, c]
        mine[c, 0] = jnp.dot(rows, w_gate[...], preferred_element_type=jnp.float32).astype(
            jnp.bfloat16
        )
        mine[c, 1] = jnp.dot(rows, w_up[...], preferred_element_type=jnp.float32).astype(
            jnp.bfloat16
        )
        mine[c, 2] = lax.dot_general(
            rows_ref[0, c], w_down[...], last, preferred_element_type=jnp.float32
        ).astype(jnp.bfloat16)
        pair_copy(c).start()

    def second_half(c):
        pair_copy(c).wait()
        gate_pre, up_pre, grad_act = (
            mine[c, i].astype(jnp.float32) + theirs[c, i].astype(jnp.float32) for i in range(3)
        )
        sigmoid_gate = 1.0 / (1.0 + jnp.exp(-gate_pre))
        swish = gate_pre * sigmoid_gate
        mine[c, 0] = (swish * up_pre).astype(jnp.bfloat16)
        mine[c, 1] = (
            grad_act * up_pre * sigmoid_gate * (1.0 + gate_pre * (1.0 - sigmoid_gate))
        ).astype(jnp.bfloat16)
        mine[c, 2] = (grad_act * swish).astype(jnp.bfloat16)
        groups = pl.ds(c * plane, plane)

        def down(i, inner):
            columns = pl.ds(pl.multiple_of(i * COLUMNS, COLUMNS), COLUMNS)
            out_rows[0, groups, :, columns] = (
                jnp.dot(mine[c, 0], w_down[:, columns], preferred_element_type=jnp.float32)
                .astype(jnp.bfloat16)
                .reshape(plane, cap, COLUMNS)
            )
            return inner

        def up(i, inner):
            columns = pl.ds(pl.multiple_of(i * COLUMNS, COLUMNS), COLUMNS)
            out_rows[1, groups, :, columns] = (
                (
                    lax.dot_general(
                        mine[c, 1], w_gate[columns, :], last, preferred_element_type=jnp.float32
                    )
                    + lax.dot_general(
                        mine[c, 2], w_up[columns, :], last, preferred_element_type=jnp.float32
                    )
                )
                .astype(jnp.bfloat16)
                .reshape(plane, cap, COLUMNS)
            )
            return inner

        lax.fori_loop(0, width // COLUMNS, down, 0)
        post(0, c)
        lax.fori_loop(0, width // COLUMNS, up, 0)
        post(1, c)

    def order(i):
        falling = Z - 1 - i - jnp.where(Z - 1 - i <= z, 1, 0)
        rising = i + jnp.where(i >= z, 1, 0)
        return jnp.where(i == Z - 1, z, jnp.where(z < Z // 2, falling, rising))

    def plane_copy(a, origin, q, sender):
        return pltpu.make_async_remote_copy(
            src_ref=out_rows.at[a, origin * plane + q],
            dst_ref=back.at[a, origin, sender],
            send_sem=send.at[a, origin, q],
            recv_sem=recv.at[a, origin, sender],
            device_id=device(z * plane + q),
            device_id_type=MESH,
        )

    def line_copy(a, way, origin):
        return pltpu.make_async_remote_copy(
            src_ref=leave.at[a, origin],
            dst_ref=inc.at[a, way, origin],
            send_sem=line_send.at[a, origin],
            recv_sem=line_recv.at[a, way, origin],
            device_id=device(me + plane - 2 * plane * way),
            device_id_type=MESH,
        )

    def post(a, origin):
        def one(d, carry):
            plane_copy(a, origin, (p + d) % plane, p).start()
            return carry

        lax.fori_loop(1, plane, one, 0)

    def gather(a, origin):
        back[a, origin, p] = out_rows[a, origin * plane + p]

        def one(d, carry):
            q = (p + d) % plane
            plane_copy(a, origin, q, q).wait_recv()
            return carry

        lax.fori_loop(1, plane, one, 0)

    def each_chunk(body):
        def chunk(c, carry):
            body(pl.ds(pl.multiple_of(c * COLUMNS, COLUMNS), COLUMNS))
            return carry

        lax.fori_loop(0, width // COLUMNS, chunk, 0)

    def partial(a, origin, columns):
        rows = back[a, origin, :, :, columns].reshape(plane * cap, COLUMNS)
        first = (((0,), (0,)), ((), ()))
        hot = hot_ref[origin]
        if a == 1:
            return lax.dot_general(hot, rows, first, preferred_element_type=jnp.float32)
        weight = hot.astype(jnp.float32) * gate_ref[origin]
        high = weight.astype(jnp.bfloat16)
        low = (weight - high.astype(jnp.float32)).astype(jnp.bfloat16)
        return lax.dot_general(
            high, rows, first, preferred_element_type=jnp.float32
        ) + lax.dot_general(low, rows, first, preferred_element_type=jnp.float32)

    def line_step(origin):
        way = jnp.where(origin > z, 0, 1)
        comes_here = jnp.where(way == 0, z, Z - 1 - z) > 0
        for a in range(2):
            gather(a, origin)

            @pl.when(comes_here)
            def _(a=a):
                line_copy(a, way, origin).wait_recv()

                @each_chunk
                def _(columns):
                    earlier = inc[a, way, origin, :, columns].astype(jnp.float32)
                    leave[a, origin, :, columns] = (
                        partial(a, origin, columns) + earlier
                    ).astype(jnp.bfloat16)

            @pl.when(jnp.logical_not(comes_here))
            def _(a=a):
                @each_chunk
                def _(columns):
                    leave[a, origin, :, columns] = partial(a, origin, columns).astype(jnp.bfloat16)

            line_copy(a, way, origin).start()

    greet(plane, True)
    comes = (z > 0, z < Z - 1)
    first_half(order(0))

    def work(i, carry):
        @pl.when(i + 1 < Z)
        def _():
            first_half(order(i + 1))

        second_half(order(i))

        @pl.when(i > 0)
        def _():
            line_step(order(i - 1))

        return carry

    lax.fori_loop(0, Z, work, 0)

    for a in range(2):
        gather(a, z)

        @each_chunk
        def _(columns, a=a):
            sum_ref[a, :, columns] = partial(a, z, columns)

    for a in range(2):
        for way in range(2):

            @pl.when(comes[way])
            def _(a=a, way=way):
                line_copy(a, way, z).wait_recv()

                @each_chunk
                def _(columns):
                    sum_ref[a, :, columns] += inc[a, way, z, :, columns].astype(jnp.float32)

    for i in range(Z - 1):
        origin = order(i)
        for a in range(2):
            line_copy(a, jnp.where(origin > z, 0, 1), origin).wait_send()

    def finish(i, carry):
        a, origin, d = i // (Z * plane), (i // plane) % Z, i % plane

        @pl.when(d > 0)
        def _():
            plane_copy(a, origin, (p + d) % plane, p).wait_send()

        return carry

    lax.fori_loop(0, 2 * Z * plane, finish, 0)


VM = pl.BlockSpec(memory_space=pltpu.VMEM)


def dispatch(attn, resid, gain, grad_out, table, plane, cap):
    tokens, width = resid.shape
    return pl.pallas_call(
        functools.partial(dispatch_kernel, plane),
        out_shape=(
            jax.ShapeDtypeStruct((2, Z * plane, cap, width), jnp.bfloat16),
            jax.ShapeDtypeStruct((tokens, width), jnp.float32),
            jax.ShapeDtypeStruct((tokens, 128), jnp.float32),
            jax.ShapeDtypeStruct((Z, plane * cap, tokens), jnp.bfloat16),
            jax.ShapeDtypeStruct((Z, plane * cap, tokens), jnp.float32),
        ),
        in_specs=[VM] * 5,
        out_specs=(VM,) * 5,
        scratch_shapes=[
            pltpu.VMEM((2, Z, tokens, width), jnp.bfloat16),
            pltpu.VMEM((2, Z, plane, cap, width), jnp.bfloat16),
            pltpu.VMEM((tokens, width), jnp.bfloat16),
            pltpu.VMEM((tokens, width), jnp.bfloat16),
            pltpu.VMEM((2, tokens, 128), jnp.float32),
            pltpu.VMEM((Z,) + table.shape, jnp.float32),
            pltpu.SemaphoreType.DMA((2, 2, Z - 1)),
            pltpu.SemaphoreType.DMA((2, 2, Z - 1)),
            pltpu.SemaphoreType.DMA((2, Z, plane)),
            pltpu.SemaphoreType.DMA((2, Z, plane)),
            pltpu.SemaphoreType.DMA((2, Z - 1)),
            pltpu.SemaphoreType.DMA((2, Z - 1)),
            pltpu.SemaphoreType.DMA((2,)),
            pltpu.SemaphoreType.DMA((2,)),
        ],
        compiler_params=pltpu.CompilerParams(
            collective_id=0, has_side_effects=True, vmem_limit_bytes=48 << 20
        ),
    )(attn, resid, gain, grad_out, table)


def combine(rows, w_gate, w_up, w_down, hot, gate, tokens, plane):
    _, groups, cap, width = rows.shape
    hidden = w_gate.shape[1]
    return pl.pallas_call(
        functools.partial(combine_kernel, plane),
        out_shape=jax.ShapeDtypeStruct((2, tokens, width), jnp.float32),
        in_specs=[VM] * 6,
        out_specs=VM,
        scratch_shapes=[
            pltpu.VMEM((2, groups, cap, width), jnp.bfloat16),
            pltpu.VMEM((Z, 3, plane * cap, hidden), jnp.bfloat16),
            pltpu.VMEM((Z, 3, plane * cap, hidden), jnp.bfloat16),
            pltpu.VMEM((2, Z, plane, cap, width), jnp.bfloat16),
            pltpu.VMEM((2, 2, Z, tokens, width), jnp.bfloat16),
            pltpu.VMEM((2, Z, tokens, width), jnp.bfloat16),
            pltpu.SemaphoreType.DMA((2, Z)),
            pltpu.SemaphoreType.DMA((2, 2, Z)),
            pltpu.SemaphoreType.DMA((2, Z, plane)),
            pltpu.SemaphoreType.DMA((2, Z, plane)),
            pltpu.SemaphoreType.DMA((Z,)),
            pltpu.SemaphoreType.DMA((Z,)),
        ],
        compiler_params=pltpu.CompilerParams(
            collective_id=1, has_side_effects=True, vmem_limit_bytes=62 << 20
        ),
    )(rows.reshape(2, Z, plane * cap, width), w_gate, w_up, w_down, hot, gate)


def row_sums(values):
    return lax.psum(jnp.sum(values, axis=1), "tensor")


def body(attn_parts, resid, norm_gain, w_gate, w_up, w_down, expert_ids, gate_weights, grad_out):
    experts = lax.axis_size("expert")
    plane = experts // Z
    tokens = expert_ids.shape[0]
    capacity = 5 * tokens * expert_ids.shape[1] // (4 * experts)
    cap = -(-capacity // 16) * 16
    width = resid.shape[1]
    table = jnp.concatenate([expert_ids.T.astype(jnp.float32), gate_weights.T], axis=0)
    rows, hidden_in, inv, hot, gate = dispatch(
        attn_parts[0], resid, norm_gain[None, :], grad_out, table, plane, cap
    )
    inv_rms = inv[:, 0]
    sums = combine(rows, w_gate[0], w_up[0], w_down[0], hot, gate, tokens, plane)
    moe, grad_normed = sums[0], sums[1]

    output = (hidden_in + moe).astype(jnp.bfloat16)
    scaled = grad_normed * norm_gain[None, :]
    inner = row_sums(hidden_in * scaled)
    grad_input = (
        grad_out.astype(jnp.float32)
        + inv_rms[:, None] * scaled
        - hidden_in * (inv_rms**3 * inner / D)[:, None]
    )
    return (output, grad_input.astype(jnp.bfloat16))


def solution(mesh):
    return jax.shard_map(
        body,
        mesh=mesh,
        in_specs=(
            P("tensor", "expert", None),
            P("expert", "tensor"),
            P("tensor"),
            P("expert", "tensor", None),
            P("expert", "tensor", None),
            P("expert", None, "tensor"),
            P("expert", None),
            P("expert", None),
            P("expert", "tensor"),
        ),
        out_specs=(P("expert", "tensor"), P("expert", "tensor")),
        check_vma=False,
    )
```

```python
import functools

import jax
import jax.numpy as jnp
from jax import lax
from jax.experimental import pallas as pl
from jax.experimental.pallas import tpu as pltpu
from jax.sharding import PartitionSpec as P

D = 4096
Z = 4
MESH = pl.DeviceIdType.MESH
COLUMNS = 512

epsilon = 1e-06


def device(expert):
    return (expert, lax.axis_index("tensor"))


def position(plane):
    me = lax.axis_index("expert")
    return me, me // plane, me % plane


def partner():
    return (lax.axis_index("expert"), 1 - lax.axis_index("tensor"))


def greet(plane, pair):
    me, z, p = position(plane)
    barrier = pltpu.get_barrier_semaphore()
    if pair:
        pl.semaphore_signal(barrier, inc=1, device_id=partner(), device_id_type=MESH)

    def hello(d, carry):
        pl.semaphore_signal(
            barrier, inc=1, device_id=device(z * plane + (p + d) % plane), device_id_type=MESH
        )
        return carry

    lax.fori_loop(1, plane, hello, 0)

    @pl.when(z > 0)
    def _():
        pl.semaphore_signal(barrier, inc=1, device_id=device(me - plane), device_id_type=MESH)

    @pl.when(z < Z - 1)
    def _():
        pl.semaphore_signal(barrier, inc=1, device_id=device(me + plane), device_id_type=MESH)

    neighbours = (z + Z - 1) // Z + (2 * Z - 2 - z) // Z
    pl.semaphore_wait(barrier, plane - 1 + int(pair) + neighbours)


def dispatch_kernel(
    plane,
    attn_ref,
    resid_ref,
    gain_ref,
    grad_ref,
    table_ref,
    rows_ref,
    hidden_ref,
    inv_ref,
    hot_ref,
    gate_ref,
    held,
    stage,
    normed,
    other,
    stat,
    tables,
    line_send,
    line_recv,
    send,
    recv,
    table_send,
    table_recv,
    pair_send,
    pair_recv,
):
    me, z, p = position(plane)
    cap, width = stage.shape[3], stage.shape[4]
    tokens = table_ref.shape[1]
    topk = table_ref.shape[0] // 2
    side = lax.axis_index("tensor")
    sources = (grad_ref, normed)

    def pair_copy(i, source, target):
        return pltpu.make_async_remote_copy(
            src_ref=source,
            dst_ref=target,
            send_sem=pair_send.at[i],
            recv_sem=pair_recv.at[i],
            device_id=partner(),
            device_id_type=MESH,
        )

    def half(of):
        return pl.ds(pl.multiple_of(of * width, width), width)

    attn_copy = pair_copy(0, attn_ref.at[:, half(1 - side)], other)
    stat_copy = pair_copy(1, stat.at[0], stat.at[1])

    def table_copy(way, step, source, origin):
        return pltpu.make_async_remote_copy(
            src_ref=source,
            dst_ref=tables.at[origin],
            send_sem=table_send.at[way, step],
            recv_sem=table_recv.at[way, step],
            device_id=device(me + plane if way == 0 else me - plane),
            device_id_type=MESH,
        )

    def find_slots(origin, table):
        count = max(16, plane)
        expert = (z * plane + lax.broadcasted_iota(jnp.int32, (count, tokens), 0)).astype(
            jnp.float32
        )
        named = jnp.zeros((count, tokens), jnp.float32)
        gates = jnp.zeros((count, tokens), jnp.float32)
        for k in range(topk):
            hit = table[k : k + 1, :] == expert
            named = jnp.where(hit, 1.0, named)
            gates = jnp.where(hit, table[topk + k : topk + k + 1, :], gates)
        before = jnp.where(
            lax.broadcasted_iota(jnp.int32, (tokens, tokens), 0)
            < lax.broadcasted_iota(jnp.int32, (tokens, tokens), 1),
            1.0,
            0.0,
        ).astype(jnp.bfloat16)
        earlier = jnp.dot(named.astype(jnp.bfloat16), before, preferred_element_type=jnp.float32)
        slot = jnp.where(named > 0.5, earlier, -1.0)
        number = lax.broadcasted_iota(jnp.int32, (cap, tokens), 0).astype(jnp.float32)
        for e in range(plane):
            own = slot[e : e + 1, :] == number
            hot_ref[origin, e * cap : (e + 1) * cap, :] = jnp.where(own, 1.0, 0.0).astype(
                jnp.bfloat16
            )
            weight = jnp.sum(jnp.where(own, gates[e : e + 1, :], 0.0), axis=1, keepdims=True)
            gate_ref[origin, e * cap : (e + 1) * cap, :] = jnp.broadcast_to(weight, (cap, tokens))

    def each_chunk(body):
        def chunk(c, carry):
            body(pl.ds(pl.multiple_of(c * COLUMNS, COLUMNS), COLUMNS))
            return carry

        lax.fori_loop(0, width // COLUMNS, chunk, 0)

    def norm():
        stat[0] = jnp.zeros((tokens, 128), jnp.float32)
        attn_copy.wait_recv()

        def chunk(c, carry):
            columns = pl.ds(pl.multiple_of(c * COLUMNS, COLUMNS), COLUMNS)
            own = pl.ds(pl.multiple_of(side * width + c * COLUMNS, COLUMNS), COLUMNS)
            value = resid_ref[:, columns].astype(jnp.float32) + (
                attn_ref[:, own].astype(jnp.float32) + other[:, columns].astype(jnp.float32)
            )
            hidden_ref[:, columns] = value
            squares = jnp.sum(value * value, axis=1, keepdims=True)
            stat[0] += jnp.broadcast_to(squares, (tokens, 128))
            return carry

        lax.fori_loop(0, width // COLUMNS, chunk, 0)
        stat_copy.start()
        stat_copy.wait_recv()
        inv_ref[...] = lax.rsqrt((stat[0] + stat[1]) / D + epsilon)

        @each_chunk
        def _(columns):
            normed[:, columns] = (
                hidden_ref[:, columns] * inv_ref[:, 0:1] * gain_ref[:, columns]
            ).astype(jnp.bfloat16)

    def line_copy(a, way, step, source, origin):
        return pltpu.make_async_remote_copy(
            src_ref=source,
            dst_ref=held.at[a, origin],
            send_sem=line_send.at[a, way, step],
            recv_sem=line_recv.at[a, way, step],
            device_id=device(me + plane if way == 0 else me - plane),
            device_id_type=MESH,
        )

    def plane_copy(a, origin, q, sender, target):
        return pltpu.make_async_remote_copy(
            src_ref=stage.at[a, origin, q],
            dst_ref=rows_ref.at[a, origin * plane + sender],
            send_sem=send.at[a, origin, q],
            recv_sem=recv.at[a, origin, sender],
            device_id=device(z * plane + target),
            device_id_type=MESH,
        )

    def spread(a, origin, block):
        @each_chunk
        def _(columns):
            picked = jnp.dot(
                hot_ref[origin], block[:, columns], preferred_element_type=jnp.float32
            )
            if a == 0:
                picked = picked * gate_ref[origin, :, 0:1]
            stage[a, origin, :, :, columns] = picked.astype(jnp.bfloat16).reshape(
                plane, cap, COLUMNS
            )

        def post(d, carry):
            q = (p + d) % plane
            plane_copy(a, origin, q, p, q).start()
            return carry

        lax.fori_loop(1, plane, post, 0)
        rows_ref[a, origin * plane + p] = stage[a, origin, p]

    greet(plane, True)
    can_go = (z < Z - 1, z > 0)
    attn_copy.start()

    def set_out(a):
        for way in range(2):

            @pl.when(can_go[way])
            def _(way=way):
                if a == 0:
                    table_copy(way, 0, table_ref, z).start()
                line_copy(a, way, 0, sources[a], z).start()

    set_out(0)
    find_slots(z, table_ref[...])
    spread(0, z, grad_ref)
    norm()
    set_out(1)
    spread(1, z, normed)
    for step in range(1, Z):
        for a in range(2):
            for way in range(2):
                origin = z - step if way == 0 else z + step
                there = z >= step if way == 0 else z + step < Z

                @pl.when(there)
                def _(a=a, way=way, step=step, origin=origin):
                    if a == 0:
                        table_copy(way, step - 1, tables.at[origin], origin).wait_recv()
                        if step < Z - 1:

                            @pl.when(can_go[way])
                            def _():
                                table_copy(way, step, tables.at[origin], origin).start()

                    line_copy(a, way, step - 1, held.at[a, origin], origin).wait_recv()
                    if step < Z - 1:

                        @pl.when(can_go[way])
                        def _():
                            line_copy(a, way, step, held.at[a, origin], origin).start()

                    if a == 0:
                        find_slots(origin, tables[origin])
                    spread(a, origin, held.at[a, origin])

    for a in range(2):
        for way in range(2):
            for step in range(Z - 1):
                origin = z - step if way == 0 else z + step
                there = z >= step if way == 0 else z + step < Z

                @pl.when(there & can_go[way])
                def _(a=a, way=way, step=step, origin=origin):
                    if a == 0:
                        table_copy(way, step, tables.at[origin], origin).wait_send()
                    line_copy(a, way, step, held.at[a, origin], origin).wait_send()

    attn_copy.wait_send()
    stat_copy.wait_send()

    def finish(i, carry):
        a, origin, d = i // (Z * plane), (i // plane) % Z, i % plane

        @pl.when(d > 0)
        def _():
            q = (p + d) % plane
            plane_copy(a, origin, q, p, q).wait_send()
            plane_copy(a, origin, q, q, q).wait_recv()

        return carry

    lax.fori_loop(0, 2 * Z * plane, finish, 0)


def combine_kernel(
    plane,
    rows_ref,
    w_gate,
    w_up,
    w_down,
    hot_ref,
    gate_ref,
    hidden_ref,
    inv_ref,
    gain_ref,
    grad_ref,
    output_ref,
    input_ref,
    sum_ref,
    stat,
    out_rows,
    mine,
    theirs,
    back,
    inc,
    leave,
    line_send,
    line_recv,
    send,
    recv,
    pair_send,
    pair_recv,
):
    me, z, p = position(plane)
    cap, width = back.shape[3], back.shape[4]
    last = (((1,), (1,)), ((), ()))

    def pair_copy(c):
        return pltpu.make_async_remote_copy(
            src_ref=mine.at[c],
            dst_ref=theirs.at[c],
            send_sem=pair_send.at[c],
            recv_sem=pair_recv.at[c],
            device_id=partner(),
            device_id_type=MESH,
        )

    def first_half(c):
        rows = rows_ref[1, c]
        mine[c, 0] = jnp.dot(rows, w_gate[...], preferred_element_type=jnp.float32).astype(
            jnp.bfloat16
        )
        mine[c, 1] = jnp.dot(rows, w_up[...], preferred_element_type=jnp.float32).astype(
            jnp.bfloat16
        )
        mine[c, 2] = lax.dot_general(
            rows_ref[0, c], w_down[...], last, preferred_element_type=jnp.float32
        ).astype(jnp.bfloat16)
        pair_copy(c).start()

    def second_half(c):
        pair_copy(c).wait()
        gate_pre, up_pre, grad_act = (
            mine[c, i].astype(jnp.float32) + theirs[c, i].astype(jnp.float32) for i in range(3)
        )
        sigmoid_gate = 1.0 / (1.0 + jnp.exp(-gate_pre))
        swish = gate_pre * sigmoid_gate
        mine[c, 0] = (swish * up_pre).astype(jnp.bfloat16)
        mine[c, 1] = (
            grad_act * up_pre * sigmoid_gate * (1.0 + gate_pre * (1.0 - sigmoid_gate))
        ).astype(jnp.bfloat16)
        mine[c, 2] = (grad_act * swish).astype(jnp.bfloat16)
        groups = pl.ds(c * plane, plane)

        def down(i, inner):
            columns = pl.ds(pl.multiple_of(i * COLUMNS, COLUMNS), COLUMNS)
            out_rows[0, groups, :, columns] = (
                jnp.dot(mine[c, 0], w_down[:, columns], preferred_element_type=jnp.float32)
                .astype(jnp.bfloat16)
                .reshape(plane, cap, COLUMNS)
            )
            return inner

        def up(i, inner):
            columns = pl.ds(pl.multiple_of(i * COLUMNS, COLUMNS), COLUMNS)
            out_rows[1, groups, :, columns] = (
                (
                    lax.dot_general(
                        mine[c, 1], w_gate[columns, :], last, preferred_element_type=jnp.float32
                    )
                    + lax.dot_general(
                        mine[c, 2], w_up[columns, :], last, preferred_element_type=jnp.float32
                    )
                )
                .astype(jnp.bfloat16)
                .reshape(plane, cap, COLUMNS)
            )
            return inner

        lax.fori_loop(0, width // COLUMNS, down, 0)
        post(0, c)
        lax.fori_loop(0, width // COLUMNS, up, 0)
        post(1, c)

    def order(i):
        falling = Z - 1 - i - jnp.where(Z - 1 - i <= z, 1, 0)
        rising = i + jnp.where(i >= z, 1, 0)
        return jnp.where(i == Z - 1, z, jnp.where(z < Z // 2, falling, rising))

    def plane_copy(a, origin, q, sender):
        return pltpu.make_async_remote_copy(
            src_ref=out_rows.at[a, origin * plane + q],
            dst_ref=back.at[a, origin, sender],
            send_sem=send.at[a, origin, q],
            recv_sem=recv.at[a, origin, sender],
            device_id=device(z * plane + q),
            device_id_type=MESH,
        )

    def place(way, origin, at):
        return jnp.where(origin == at, origin + (Z - origin) * way, origin)

    def line_copy(a, way, origin, at):
        return pltpu.make_async_remote_copy(
            src_ref=leave.at[a, origin],
            dst_ref=inc.at[a, place(way, origin, at)],
            send_sem=line_send.at[a, origin],
            recv_sem=line_recv.at[a, way, origin],
            device_id=device(me + plane - 2 * plane * way),
            device_id_type=MESH,
        )

    def post(a, origin):
        def one(d, carry):
            plane_copy(a, origin, (p + d) % plane, p).start()
            return carry

        lax.fori_loop(1, plane, one, 0)

    def gather(a, origin):
        back[a, origin, p] = out_rows[a, origin * plane + p]

        def one(d, carry):
            q = (p + d) % plane
            plane_copy(a, origin, q, q).wait_recv()
            return carry

        lax.fori_loop(1, plane, one, 0)

    def each_chunk(body):
        def chunk(c, carry):
            body(pl.ds(pl.multiple_of(c * COLUMNS, COLUMNS), COLUMNS))
            return carry

        lax.fori_loop(0, width // COLUMNS, chunk, 0)

    def partial(a, origin, columns):
        rows = back[a, origin, :, :, columns].reshape(plane * cap, COLUMNS)
        first = (((0,), (0,)), ((), ()))
        hot = hot_ref[origin]
        if a == 1:
            return lax.dot_general(hot, rows, first, preferred_element_type=jnp.float32)
        weight = hot.astype(jnp.float32) * gate_ref[origin]
        high = weight.astype(jnp.bfloat16)
        low = (weight - high.astype(jnp.float32)).astype(jnp.bfloat16)
        return lax.dot_general(
            high, rows, first, preferred_element_type=jnp.float32
        ) + lax.dot_general(low, rows, first, preferred_element_type=jnp.float32)

    def line_step(origin):
        way = jnp.where(origin > z, 0, 1)
        comes_here = jnp.where(way == 0, z, Z - 1 - z) > 0
        for a in range(2):
            gather(a, origin)

            @pl.when(comes_here)
            def _(a=a):
                line_copy(a, way, origin, z).wait_recv()

                @each_chunk
                def _(columns):
                    earlier = inc[a, origin, :, columns].astype(jnp.float32)
                    leave[a, origin, :, columns] = (
                        partial(a, origin, columns) + earlier
                    ).astype(jnp.bfloat16)

            @pl.when(jnp.logical_not(comes_here))
            def _(a=a):
                @each_chunk
                def _(columns):
                    leave[a, origin, :, columns] = partial(a, origin, columns).astype(jnp.bfloat16)

            line_copy(a, way, origin, z + 1 - 2 * way).start()

    greet(plane, True)
    comes = (z > 0, z < Z - 1)
    first_half(order(0))

    def work(i, carry):
        second_half(order(i))

        @pl.when(i + 1 < Z)
        def _():
            first_half(order(i + 1))

        @pl.when(i > 0)
        def _():
            line_step(order(i - 1))

        return carry

    lax.fori_loop(0, Z, work, 0)

    for a in range(2):
        gather(a, z)

        @each_chunk
        def _(columns, a=a):
            sum_ref[a, :, columns] = partial(a, z, columns)

    for a in range(2):
        for way in range(2):

            @pl.when(comes[way])
            def _(a=a, way=way):
                line_copy(a, way, z, z).wait_recv()

                @each_chunk
                def _(columns):
                    sum_ref[a, :, columns] += inc[a, z if way == 0 else Z, :, columns].astype(jnp.float32)

    stat_copy = pltpu.make_async_remote_copy(
        src_ref=stat.at[0],
        dst_ref=stat.at[1],
        send_sem=pair_send.at[Z],
        recv_sem=pair_recv.at[Z],
        device_id=partner(),
        device_id_type=MESH,
    )
    stat[0] = jnp.zeros(inv_ref.shape, jnp.float32)

    @each_chunk
    def _(columns):
        scaled = sum_ref[1, :, columns] * gain_ref[:, columns]
        sum_ref[1, :, columns] = scaled
        inner = jnp.sum(hidden_ref[:, columns] * scaled, axis=1, keepdims=True)
        stat[0] += jnp.broadcast_to(inner, inv_ref.shape)

    stat_copy.start()

    @each_chunk
    def _(columns):
        output_ref[:, columns] = (hidden_ref[:, columns] + sum_ref[0, :, columns]).astype(
            jnp.bfloat16
        )

    stat_copy.wait()
    inv_rms = inv_ref[...]
    stat[0] = inv_rms * inv_rms * inv_rms * (stat[0] + stat[1]) / D

    @each_chunk
    def _(columns):
        input_ref[:, columns] = (
            grad_ref[:, columns].astype(jnp.float32)
            + inv_ref[:, 0:1] * sum_ref[1, :, columns]
            - hidden_ref[:, columns] * stat[0, :, 0:1]
        ).astype(jnp.bfloat16)

    for i in range(Z - 1):
        origin = order(i)
        for a in range(2):
            line_copy(a, jnp.where(origin > z, 0, 1), origin, z).wait_send()

    def finish(i, carry):
        a, origin, d = i // (Z * plane), (i // plane) % Z, i % plane

        @pl.when(d > 0)
        def _():
            plane_copy(a, origin, (p + d) % plane, p).wait_send()

        return carry

    lax.fori_loop(0, 2 * Z * plane, finish, 0)


VM = pl.BlockSpec(memory_space=pltpu.VMEM)


def dispatch(attn, resid, gain, grad_out, table, plane, cap):
    tokens, width = resid.shape
    return pl.pallas_call(
        functools.partial(dispatch_kernel, plane),
        out_shape=(
            jax.ShapeDtypeStruct((2, Z * plane, cap, width), jnp.bfloat16),
            jax.ShapeDtypeStruct((tokens, width), jnp.float32),
            jax.ShapeDtypeStruct((tokens, 128), jnp.float32),
            jax.ShapeDtypeStruct((Z, plane * cap, tokens), jnp.bfloat16),
            jax.ShapeDtypeStruct((Z, plane * cap, tokens), jnp.float32),
        ),
        in_specs=[VM] * 5,
        out_specs=(VM,) * 5,
        scratch_shapes=[
            pltpu.VMEM((2, Z, tokens, width), jnp.bfloat16),
            pltpu.VMEM((2, Z, plane, cap, width), jnp.bfloat16),
            pltpu.VMEM((tokens, width), jnp.bfloat16),
            pltpu.VMEM((tokens, width), jnp.bfloat16),
            pltpu.VMEM((2, tokens, 128), jnp.float32),
            pltpu.VMEM((Z,) + table.shape, jnp.float32),
            pltpu.SemaphoreType.DMA((2, 2, Z - 1)),
            pltpu.SemaphoreType.DMA((2, 2, Z - 1)),
            pltpu.SemaphoreType.DMA((2, Z, plane)),
            pltpu.SemaphoreType.DMA((2, Z, plane)),
            pltpu.SemaphoreType.DMA((2, Z - 1)),
            pltpu.SemaphoreType.DMA((2, Z - 1)),
            pltpu.SemaphoreType.DMA((2,)),
            pltpu.SemaphoreType.DMA((2,)),
        ],
        compiler_params=pltpu.CompilerParams(
            collective_id=0, has_side_effects=True, vmem_limit_bytes=48 << 20
        ),
    )(attn, resid, gain, grad_out, table)


def combine(rows, w_gate, w_up, w_down, hot, gate, hidden_in, inv, gain, grad_out, plane):
    _, groups, cap, width = rows.shape
    hidden = w_gate.shape[1]
    tokens = grad_out.shape[0]
    return pl.pallas_call(
        functools.partial(combine_kernel, plane),
        out_shape=(jax.ShapeDtypeStruct((tokens, width), jnp.bfloat16),) * 2,
        in_specs=[VM] * 10,
        out_specs=(VM,) * 2,
        scratch_shapes=[
            pltpu.VMEM((2, tokens, width), jnp.float32),
            pltpu.VMEM((2, tokens, 128), jnp.float32),
            pltpu.VMEM((2, groups, cap, width), jnp.bfloat16),
            pltpu.VMEM((Z, 3, plane * cap, hidden), jnp.bfloat16),
            pltpu.VMEM((Z, 3, plane * cap, hidden), jnp.bfloat16),
            pltpu.VMEM((2, Z, plane, cap, width), jnp.bfloat16),
            pltpu.VMEM((2, Z + 1, tokens, width), jnp.bfloat16),
            pltpu.VMEM((2, Z, tokens, width), jnp.bfloat16),
            pltpu.SemaphoreType.DMA((2, Z)),
            pltpu.SemaphoreType.DMA((2, 2, Z)),
            pltpu.SemaphoreType.DMA((2, Z, plane)),
            pltpu.SemaphoreType.DMA((2, Z, plane)),
            pltpu.SemaphoreType.DMA((Z + 1,)),
            pltpu.SemaphoreType.DMA((Z + 1,)),
        ],
        compiler_params=pltpu.CompilerParams(
            collective_id=1, has_side_effects=True, vmem_limit_bytes=62 << 20
        ),
    )(rows.reshape(2, Z, plane * cap, width), w_gate, w_up, w_down, hot, gate, hidden_in, inv, gain, grad_out)


def body(attn_parts, resid, norm_gain, w_gate, w_up, w_down, expert_ids, gate_weights, grad_out):
    experts = lax.axis_size("expert")
    plane = experts // Z
    tokens = expert_ids.shape[0]
    capacity = 5 * tokens * expert_ids.shape[1] // (4 * experts)
    cap = -(-capacity // 16) * 16
    width = resid.shape[1]
    table = jnp.concatenate([expert_ids.T.astype(jnp.float32), gate_weights.T], axis=0)
    rows, hidden_in, inv, hot, gate = dispatch(
        attn_parts[0], resid, norm_gain[None, :], grad_out, table, plane, cap
    )
    return combine(
        rows,
        w_gate[0],
        w_up[0],
        w_down[0],
        hot,
        gate,
        hidden_in,
        inv,
        norm_gain[None, :],
        grad_out,
        plane,
    )


def solution(mesh):
    return jax.shard_map(
        body,
        mesh=mesh,
        in_specs=(
            P("tensor", "expert", None),
            P("expert", "tensor"),
            P("tensor"),
            P("expert", "tensor", None),
            P("expert", "tensor", None),
            P("expert", None, "tensor"),
            P("expert", None),
            P("expert", None),
            P("expert", "tensor"),
        ),
        out_specs=(P("expert", "tensor"), P("expert", "tensor")),
        check_vma=False,
    )
```
